32 devices in a mesh: proto: 8 (over y, x, core), batch: 4 (over z).
Axes of the slice: x: 2, y: 2, z: 4, core: 2. Of those that a mesh axis runs over, the one named last changes fastest.
Arguments:
- student_patches: bfloat16 [5120, 256], P('batch'), may hold values from -0.5 to 0.5
- teacher_patches: bfloat16 [5120, 256], P('batch'), may hold values from -0.5 to 0.5
- positions: int32 [2560], P('batch'), may hold values from 0 to 5119, as said below
- token_weight: float32 [2560], P('batch'), may hold values from 4 to 32
- student_protos: bfloat16 [16384, 256], P('proto'), may hold values from -0.1 to 0.1
- teacher_protos: bfloat16 [16384, 256], P('proto'), may hold values from -0.5 to 0.5
Outputs:
- patch_grad: bfloat16 [5120, 256], P('batch')
- proto_grad: bfloat16 [16384, 256], P('proto')
The draws below stay inside these ranges and needn't reach their ends.
Inputs may be any that keep to these rules, and one draw needn't show every extreme that they name: `positions`: the j-th block of 640 entries holds 640 different indices among patches j * 1280 to (j + 1) * 1280 - 1; the first and last patch of each such block are always among them.
All inputs are finite; a program needn't handle non-finite values.
Results may differ from the reference program's by a relative error of at most 0.001.
The reference program's roundings to bfloat16 on the way (of `coefficient`) count: a program that leaves them out, or rounds other values in their place, can miss the bound.
Values may be sent and summed in bfloat16 or wider, within the bound.
A program may use at most 64 MiB of HBM per device.

```python
import math
import jax
import jax.numpy as jnp
from jax import lax

D = 256
PROTO_DEV = 2048
PROTOS = 16384
TOK_DEV = 640
TOKENS = 2560
PATCH_DEV = 1280
PATCHES = 5120
ITERS = 3


def shared_basis(key, salt_value):
    return jax.random.normal(jax.random.fold_in(key, salt_value), (4, D), jnp.float32) * D ** (-0.5)


def mixed_rows(directions, loadings, jitter):
    combined = jitter
    for column in range(4):
        combined = combined + loadings[:, column:column + 1] * directions[column][None, :]
    return combined


def draw_positions(key, part):
    key = jax.random.fold_in(key, 11)
    count_blocks = TOKENS // TOK_DEV

    def single_block(block_index):
        sub_key = jax.random.fold_in(key, block_index)
        middle = jax.random.permutation(jax.random.fold_in(sub_key, 1), PATCH_DEV - 2)[:TOK_DEV - 2] + 1
        chosen = jnp.concatenate([jnp.array([0, PATCH_DEV - 1], jnp.int32), middle.astype(jnp.int32)])
        shuffle = jax.random.permutation(jax.random.fold_in(sub_key, 2), TOK_DEV)
        return chosen[shuffle] + block_index * PATCH_DEV
    return jax.vmap(single_block)(jnp.arange(count_blocks, dtype=jnp.int32)).reshape(TOKENS).astype(jnp.int32)


def draw_teacher_patches(key, part):
    directions = shared_basis(key, 101)
    key = jax.random.fold_in(key, 3)
    random_seeds = jax.random.split(key, 6)
    count_blocks = PATCHES // PATCH_DEV
    global_logits = jax.random.uniform(random_seeds[0], (8,), jnp.float32, 0.0, math.log(6.0))
    block_logits = jax.random.uniform(random_seeds[1], (count_blocks, 8), jnp.float32, 0.0, math.log(6.0))
    row_logits = jnp.repeat(global_logits[None, :] + block_logits, PATCH_DEV, axis=0, total_repeat_length=PATCHES)
    kind = jax.random.categorical(random_seeds[2], row_logits, axis=-1)
    chosen = jnp.take(directions, kind % 4, axis=0)
    polarity = jnp.where(kind < 4, 1.0, -1.0)
    block_multiplier = jnp.exp(jax.random.uniform(random_seeds[3], (count_blocks,), jnp.float32, math.log(0.7), math.log(1.5)))
    strength = jnp.exp(jax.random.uniform(random_seeds[4], (PATCHES,), jnp.float32, math.log(0.6), math.log(1.5)))
    jitter = jax.random.normal(random_seeds[5], (PATCHES, D), jnp.float32) * (0.5 * D ** (-0.5))
    amplitude = polarity * strength * jnp.repeat(block_multiplier, PATCH_DEV, total_repeat_length=PATCHES)
    features = amplitude[:, None] * chosen + jitter
    return jnp.clip(features, -0.5, 0.5).astype(jnp.bfloat16)


def draw_teacher_protos(key, part):
    directions = shared_basis(key, 101)
    key = jax.random.fold_in(key, 5)
    random_seeds = jax.random.split(key, 3)
    block_multiplier = jnp.exp(jax.random.uniform(random_seeds[0], (PROTOS // PROTO_DEV,), jnp.float32, math.log(0.6), math.log(1.4)))
    loadings = jax.random.normal(random_seeds[1], (PROTOS, 4), jnp.float32)
    jitter = jax.random.normal(random_seeds[2], (PROTOS, D), jnp.float32) * (0.5 * D ** (-0.5))
    loadings = loadings * jnp.repeat(block_multiplier, PROTO_DEV, total_repeat_length=PROTOS)[:, None]
    features = mixed_rows(directions, loadings, jitter)
    return jnp.clip(features, -0.5, 0.5).astype(jnp.bfloat16)


def draw_student_patches(key, part):
    directions = shared_basis(key, 202)
    key = jax.random.fold_in(key, 7)
    random_seeds = jax.random.split(key, 5)
    cluster = jax.random.randint(random_seeds[0], (PATCHES,), 0, 4)
    chosen = jnp.take(directions, cluster, axis=0)
    flipped = jnp.where(jax.random.randint(random_seeds[1], (PATCHES,), 0, 2) == 1, 1.0, -1.0)
    strength = jnp.exp(jax.random.uniform(random_seeds[2], (PATCHES,), jnp.float32, math.log(1.5), math.log(3.0)))
    row_gain = jnp.exp(jax.random.uniform(random_seeds[3], (PATCHES,), jnp.float32, math.log(0.4), math.log(4.0)))
    jitter = jax.random.normal(random_seeds[4], (PATCHES, D), jnp.float32) * D ** (-0.5)
    amplitude = flipped * strength
    factor = 0.02 * D ** 0.5 * row_gain / jnp.sqrt(1.0 + amplitude * amplitude)
    features = (amplitude[:, None] * chosen + jitter) * factor[:, None]
    return jnp.clip(features, -0.5, 0.5).astype(jnp.bfloat16)


def draw_student_protos(key, part):
    directions = shared_basis(key, 202)
    key = jax.random.fold_in(key, 9)
    random_seeds = jax.random.split(key, 3)
    loadings = jax.random.normal(random_seeds[0], (PROTOS, 4), jnp.float32) * 0.6
    row_gain = jnp.exp(jax.random.uniform(random_seeds[1], (PROTOS,), jnp.float32, math.log(0.4), math.log(4.0)))
    jitter = jax.random.normal(random_seeds[2], (PROTOS, D), jnp.float32) * D ** (-0.5)
    length = jnp.sqrt(1.0 + jnp.sum(loadings * loadings, axis=1))
    factor = 0.004 * D ** 0.5 * row_gain / length
    features = mixed_rows(directions, loadings, jitter) * factor[:, None]
    return jnp.clip(features, -0.1, 0.1).astype(jnp.bfloat16)


def steps_of(own_key, extent, pieces, smallest, high):
    def one(dim, parts):
        heights = jax.random.uniform(jax.random.fold_in(jax.random.fold_in(own_key, 6), dim), (parts,), jnp.float32, smallest / len(pieces), high / len(pieces))
        return jnp.repeat(jnp.exp(heights), extent[dim] // parts).reshape((-1,) + (1,) * (len(extent) - dim - 1))

    gain = one(*pieces[0])
    for cut in pieces[1:]:
        gain = gain * one(*cut)
    return gain


def setup_inputs(seed: int = 0) -> dict:
    arg_keys = jax.random.split(jax.random.key(seed), 7)
    student_patches = draw_student_patches(jax.random.fold_in(arg_keys[6], 71), 0)
    teacher_patches = draw_teacher_patches(jax.random.fold_in(arg_keys[6], 71), 0)
    positions = draw_positions(jax.random.fold_in(arg_keys[6], 71), 0)
    token_weight = jnp.clip(jnp.exp(math.log(32.0) - 2.0794415 * jax.random.uniform(arg_keys[3], (TOKENS,), jnp.float32) ** steps_of(arg_keys[3], (TOKENS,), ((0, 4),), -0.2, 0.2)), 4.0, 32.0)
    student_protos = draw_student_protos(jax.random.fold_in(arg_keys[6], 71), 0)
    teacher_protos = draw_teacher_protos(jax.random.fold_in(arg_keys[6], 71), 0)
    return dict(student_patches=student_patches, teacher_patches=teacher_patches, positions=positions, token_weight=token_weight, student_protos=student_protos, teacher_protos=teacher_protos)


TEMP_TEACHER = 0.07
TEMP_STUDENT = 0.1
LENGTH_FLOOR = 1e-12

def unit_rows(transport_plan):
    values = transport_plan.astype(jnp.float32)
    row_norms = jnp.sqrt(lax.optimization_barrier(jnp.sum(values * values, axis=1, keepdims=True)) + LENGTH_FLOOR)
    return (values / row_norms, row_norms)

def reference(student_patches, teacher_patches, positions, token_weight, student_protos, teacher_protos):
    student_unit, student_norm = unit_rows(student_patches[positions])
    teacher_unit, unused_norm = unit_rows(teacher_patches[positions])
    student_half = student_unit.astype(jnp.bfloat16)
    teacher_half = teacher_unit.astype(jnp.bfloat16)
    proto_unit, proto_norm = unit_rows(student_protos)
    proto_half = proto_unit.astype(jnp.bfloat16)
    target_unit, unused_target = unit_rows(teacher_protos)
    target_half = target_unit.astype(jnp.bfloat16)
    count_blocks = PROTOS // PROTO_DEV
    proto_blocks = proto_half.reshape(count_blocks, PROTO_DEV, D)
    target_blocks = target_half.reshape(count_blocks, PROTO_DEV, D)

    def teacher_exp(proto_block):
        return jnp.exp(jnp.dot(teacher_half, proto_block.T, preferred_element_type=jnp.float32) / TEMP_TEACHER)

    def student_exp(proto_block):
        return jnp.exp(jnp.dot(student_half, proto_block.T, preferred_element_type=jnp.float32) / TEMP_STUDENT)
    row_scale = jnp.ones((TOKENS,), jnp.float32)
    col_scale = jnp.zeros((count_blocks, PROTO_DEV), jnp.float32)
    for iteration in range(ITERS):

        def sweep_block(running, proto_block):
            exponent = teacher_exp(proto_block)
            column = 1.0 / lax.optimization_barrier(jnp.sum(row_scale[:, None] * exponent, axis=0))
            return (running + lax.optimization_barrier(jnp.sum(exponent * column[None, :], axis=1)), column)
        row_total, col_scale = lax.scan(sweep_block, jnp.zeros((TOKENS,), jnp.float32), target_blocks)
        row_scale = row_scale / (row_scale * row_total)

    def student_block(running, proto_block):
        return (running + lax.optimization_barrier(jnp.sum(student_exp(proto_block), axis=1)), None)
    student_total, unused = lax.scan(student_block, jnp.zeros((TOKENS,), jnp.float32), proto_blocks)

    def grad_block(running, inputs):
        proto_block, target_block, column = inputs
        probability = student_exp(proto_block) / student_total[:, None]
        target = row_scale[:, None] * teacher_exp(target_block) * column[None, :]
        coefficient = (token_weight[:, None] * (probability - target) / TEMP_STUDENT).astype(jnp.bfloat16)
        running = running + jnp.dot(coefficient, proto_block, preferred_element_type=jnp.float32)
        proto_term = jnp.dot(coefficient.T, student_half, preferred_element_type=jnp.float32)
        return (running, proto_term)
    feature_total, proto_terms = lax.scan(grad_block, jnp.zeros((TOKENS, D), jnp.float32), (proto_blocks, target_blocks, col_scale))
    inner_product = lax.optimization_barrier(jnp.sum(feature_total * student_unit, axis=1, keepdims=True))
    feature_grad = (feature_total - inner_product * student_unit) / student_norm
    patch_grad = jnp.zeros((PATCHES, D), jnp.float32).at[positions].set(feature_grad).astype(jnp.bfloat16)
    proto_total = proto_terms.reshape(PROTOS, D)
    proto_inner = lax.optimization_barrier(jnp.sum(proto_total * proto_unit, axis=1, keepdims=True))
    proto_grad = ((proto_total - proto_inner * proto_unit) / proto_norm).astype(jnp.bfloat16)
    return (patch_grad, proto_grad)
```

```python
import functools
import math

import jax
import jax.numpy as jnp
from jax import lax
from jax.experimental import pallas as pl
from jax.experimental.pallas import tpu as pltpu
from jax.sharding import PartitionSpec as P

ITERS = 3
TEMP_TEACHER = 0.07
TEMP_STUDENT = 0.1
LENGTH_FLOOR = 1e-12
LOG2E = math.log2(math.e)
TEACHER_RATE = LOG2E / TEMP_TEACHER
STUDENT_RATE = LOG2E / TEMP_STUDENT
GROUP = 8
TILE = 256
LANES = 128
MESH = pl.DeviceIdType.MESH
F32 = jnp.float32
BF16 = jnp.bfloat16


def dot_nt(a, b):
    return lax.dot_general(a, b, (((1,), (1,)), ((), ())), preferred_element_type=F32)


def dot_nn(a, b):
    return jnp.dot(a, b, preferred_element_type=F32)


def row_norm(values):
    return jnp.sqrt(jnp.sum(values * values, axis=1, keepdims=True) + LENGTH_FLOOR)


def as_columns(row):
    return jnp.transpose(jnp.broadcast_to(row, (LANES, row.shape[1])))


def kernel(
    n_p, n_z,
    sp, tp, pos, weight, pp, qp,
    patch_out, proto_out,
    hot, tok, s_unit, s_norm, ph, qh, e_ref, s_ref, acc_ref, acc2_ref,
    rb_ref, ab_ref, cb_ref, crow_ref,
    row_buf, col_buf, fac_buf, feat, rs_buf, rs2_buf, fgrad,
    row_send, row_recv, col_send, col_recv, fac_send, fac_recv,
    t1_send, t1_recv, t2_send, t2_recv, t3_send, t3_recv,
    rs_send, rs_recv, rs2_send, rs2_recv, ag_send, ag_recv,
):
    tokens = tok.shape[1]
    patches, dim = sp.shape
    protos = pp.shape[0]
    share = tokens // GROUP
    octets = n_p // GROUP
    me_p = lax.axis_index("proto")
    me_z = lax.axis_index("batch")
    octet = me_p // GROUP
    g = me_p % GROUP

    def rows_of(member):
        return pl.multiple_of(((member % 2) * (GROUP // 2) + member // 2) * share, 16)

    barrier = pltpu.get_barrier_semaphore()
    for j in range(1, n_p):
        pl.semaphore_signal(barrier, inc=1, device_id=((me_p + j) % n_p, me_z), device_id_type=MESH)
    for j in range(1, n_z):
        pl.semaphore_signal(barrier, inc=1, device_id=(me_p, (me_z + j) % n_z), device_id_type=MESH)

    def remote(src, dst, send, recv, p, z):
        return pltpu.make_async_remote_copy(
            src_ref=src, dst_ref=dst, send_sem=send, recv_sem=recv,
            device_id=(p, z), device_id_type=MESH,
        )

    def row_copies(it):
        mine = row_buf.at[it, me_p]
        return [
            remote(mine, mine, row_send.at[it, j - 1], row_recv.at[it, j - 1], (me_p + j) % n_p, me_z)
            for j in range(1, n_p)
        ]

    def col_copies(it):
        mine = col_buf.at[it, me_z]
        return [
            remote(mine, mine, col_send.at[it, j - 1], col_recv.at[it, j - 1], me_p, (me_z + j) % n_z)
            for j in range(1, n_z)
        ]

    def start(copies):
        for copy in copies:
            copy.start()

    def wait(copies):
        for copy in copies:
            copy.wait()

    local = pos[...] - me_z * patches
    local_col = as_columns(local.astype(F32))
    lane = lax.broadcasted_iota(jnp.int32, (tokens, LANES), 1).astype(F32)
    for t in range(patches // LANES):
        hot[:, t * LANES:(t + 1) * LANES] = jnp.where(
            local_col == lane + float(t * LANES), 1.0, 0.0
        ).astype(BF16)

    @pl.loop(0, tokens // LANES)
    def _(i):
        rows = pl.ds(pl.multiple_of(i * LANES, LANES), LANES)
        picked = hot[rows, :]
        student = dot_nn(picked, sp[...])
        norm = row_norm(student)
        unit = student / norm
        s_unit[rows, :] = unit
        s_norm[rows, :] = jnp.broadcast_to(norm, (LANES, LANES))
        teacher = dot_nn(picked, tp[...])
        tok[me_z, rows, 0:dim] = unit.astype(BF16)
        tok[me_z, rows, dim:2 * dim] = (teacher / row_norm(teacher)).astype(BF16)

    @pl.loop(0, protos // TILE)
    def _(i):
        rows = pl.ds(pl.multiple_of(i * TILE, TILE), TILE)
        values = qp[rows, :].astype(F32)
        half = (values / row_norm(values)).astype(BF16)
        qh[rows, :] = half
        exps = jnp.exp2(dot_nt(tok[me_z, :, dim:2 * dim], half) * TEACHER_RATE)
        e_ref[:, rows] = exps
        col_buf[0, me_z, :, rows] = jnp.sum(exps, axis=0, keepdims=True)

    pl.semaphore_wait(barrier, n_p + n_z - 2)
    copies = col_copies(0)
    start(copies)

    acc2_ref[...] = jnp.zeros_like(acc2_ref)

    @pl.loop(0, protos // TILE)
    def _(i):
        rows = pl.ds(pl.multiple_of(i * TILE, TILE), TILE)
        values = pp[rows, :].astype(F32)
        half = (values / row_norm(values)).astype(BF16)
        ph[rows, :] = half
        exps = jnp.exp2(dot_nt(tok[me_z, :, 0:dim], half) * STUDENT_RATE)
        s_ref[:, rows] = exps
        acc2_ref[...] += exps[:, 0:LANES] + exps[:, LANES:2 * LANES]

    def lane_sums(ref):
        return jnp.sum(jnp.transpose(ref[...]), axis=0, keepdims=True)

    t1 = []
    for j in range(1, n_z):
        block = tok.at[me_z, pl.ds(rows_of(g), share), :]
        t1.append(remote(block, block, t1_send.at[j - 1], t1_recv.at[j - 1], me_p, (me_z + j) % n_z))
    t2 = []
    t3 = []
    other = me_p + 1 - 2 * (me_p % 2)
    for j in range(1, n_z):
        source = (me_z + n_z - j) % n_z
        block = tok.at[source, pl.ds(rows_of(g), share), :]
        for k in range(1, GROUP // 2):
            t2.append(remote(
                block, block, t2_send.at[j - 1, k - 1], t2_recv.at[j - 1, k - 1],
                octet * GROUP + (g + 2 * k) % GROUP, me_z,
            ))
        half_rows = pl.ds(pl.multiple_of((g % 2) * (tokens // 2), 16), tokens // 2)
        block = tok.at[source, half_rows, :]
        t3.append(remote(block, block, t3_send.at[j - 1], t3_recv.at[j - 1], other, me_z))

    row_scale = jnp.ones((1, tokens), F32)
    student_total = None
    for it in range(ITERS):
        if it > 0:
            def col_step(i, carry):
                rows = pl.ds(pl.multiple_of(i * 32, 32), 32)
                scale = rb_ref[rows, :]
                out = []
                for t in range(protos // LANES):
                    part = e_ref[rows, t * LANES:(t + 1) * LANES] * scale
                    out.append(carry[t] + jnp.sum(part.reshape(4, 8, LANES), axis=0))
                return tuple(out)
            sums = lax.fori_loop(
                0, tokens // 32, col_step,
                tuple(jnp.zeros((8, LANES), F32) for _ in range(protos // LANES)),
            )
            for t in range(protos // LANES):
                col_buf[it, me_z, :, t * LANES:(t + 1) * LANES] = jnp.sum(sums[t], axis=0, keepdims=True)
            copies = col_copies(it)
            start(copies)
        wait(copies)
        if it == 0:
            start(t1)
        total = col_buf[it, 0]
        for q in range(1, n_z):
            total = total + col_buf[it, q]
        crow_ref[...] = 1.0 / total

        @pl.loop(0, tokens // 64)
        def _(i):
            rows = pl.ds(pl.multiple_of(i * 64, 64), 64)
            running = e_ref[rows, 0:LANES] * crow_ref[:, 0:LANES]
            for t in range(1, protos // LANES):
                cols = slice(t * LANES, (t + 1) * LANES)
                running = running + e_ref[rows, cols] * crow_ref[:, cols]
            acc_ref[rows, :] = running

        row_buf[it, me_p, 0:1, :] = lane_sums(acc_ref)
        row_buf[it, me_p, 1:2, :] = lane_sums(acc2_ref)
        copies = row_copies(it)
        start(copies)
        if it == ITERS - 1:
            cb_ref[...] = as_columns(crow_ref[...])
        wait(copies)
        if it == 1:
            wait(t1)
            start(t2)
        total = row_buf[it, 0]
        for q in range(1, n_p):
            total = total + row_buf[it, q]
        row_scale = row_scale / (row_scale * total[0:1, :])
        student_total = total[1:2, :]
        if it < ITERS - 1:
            rb_ref[...] = as_columns(row_scale)

    gain = weight[...] / TEMP_STUDENT
    student_gain = gain / student_total
    teacher_gain = gain * row_scale
    fac_buf[me_z, 0:1, :] = student_gain
    fac_buf[me_z, 1:2, :] = teacher_gain
    mine = fac_buf.at[me_z]
    fac = [
        remote(mine, mine, fac_send.at[j - 1], fac_recv.at[j - 1], me_p, (me_z + j) % n_z)
        for j in range(1, n_z)
    ]
    start(fac)
    wait(t2)
    start(t3)

    rb_ref[...] = as_columns(teacher_gain)
    ab_ref[...] = as_columns(student_gain)

    @pl.loop(0, tokens // LANES)
    def _(i):
        rows = pl.ds(pl.multiple_of(i * LANES, LANES), LANES)
        a = ab_ref[rows, :]
        b = rb_ref[rows, :]
        parts = []
        for t in range(protos // LANES):
            cols = slice(t * LANES, (t + 1) * LANES)
            parts.append(
                (s_ref[rows, cols] * a - e_ref[rows, cols] * b * crow_ref[:, cols]).astype(BF16)
            )
        feat[rows, :] = dot_nn(jnp.concatenate(parts, axis=1), ph[...])

    rs = []
    for j in range(1, GROUP):
        to = (g + j) % GROUP
        rs.append(remote(
            feat.at[pl.ds(rows_of(to), share), :], rs_buf.at[j - 1],
            rs_send.at[j - 1], rs_recv.at[j - 1], octet * GROUP + to, me_z,
        ))
    start(rs)
    wait(fac)
    wait(t3)

    def proto_tile(i):
        rows = pl.ds(pl.multiple_of(i * TILE, TILE), TILE)
        p_half = ph[rows, :]
        q_half = qh[rows, :]
        c = jnp.concatenate([cb_ref[rows, :]] * (tokens // LANES), axis=1)

        def block(z, running):
            student = tok[z, :, 0:dim]
            prob = jnp.exp2(dot_nt(p_half, student) * STUDENT_RATE)
            target = jnp.exp2(dot_nt(q_half, tok[z, :, dim:2 * dim]) * TEACHER_RATE)
            coefficient = prob * fac_buf[z, 0:1, :] - target * fac_buf[z, 1:2, :] * c
            return running + dot_nn(coefficient.astype(BF16), student)

        total = jnp.zeros((TILE, dim), F32)
        if n_z <= 4:
            for z in range(n_z):
                total = block(z, total)
        else:
            total = lax.fori_loop(0, n_z, block, total)
        values = pp[rows, :].astype(F32)
        norm = row_norm(values)
        unit = values / norm
        inner = jnp.sum(total * unit, axis=1, keepdims=True)
        proto_out[rows, :] = ((total - inner * unit) / norm).astype(BF16)

    tiles = protos // TILE
    early = tiles - 3
    pl.loop(0, early)(proto_tile)

    wait(rs)
    own = pl.ds(rows_of(g), share)
    total = feat[own, :]
    for j in range(1, GROUP):
        total = total + rs_buf[j - 1]
    if octets > 1:
        rs2_buf[octet] = total
        mine2 = rs2_buf.at[octet]
        rs2 = [
            remote(mine2, mine2, rs2_send.at[j - 1], rs2_recv.at[j - 1],
                   ((octet + j) % octets) * GROUP + g, me_z)
            for j in range(1, octets)
        ]
        start(rs2)
        wait(rs2)
        total = rs2_buf[0]
        for q in range(1, octets):
            total = total + rs2_buf[q]
    unit = s_unit[own, :]
    inner = jnp.sum(total * unit, axis=1, keepdims=True)
    norm = jnp.concatenate([s_norm[own, :]] * (dim // LANES), axis=1)
    fgrad[own, :] = ((total - inner * unit) / norm).astype(BF16)
    piece = fgrad.at[own, :]
    ag = [
        remote(piece, piece, ag_send.at[j - 1], ag_recv.at[j - 1],
               octet * GROUP + (g + j) % GROUP, me_z)
        for j in range(1, GROUP)
    ]
    start(ag)

    pl.loop(early, tiles)(proto_tile)

    wait(ag)

    @pl.loop(0, patches // TILE)
    def _(i):
        rows = pl.ds(pl.multiple_of(i * TILE, TILE), TILE)
        index = lax.broadcasted_iota(jnp.int32, (TILE, tokens), 0) + i * TILE
        chosen = jnp.where(index == local, 1.0, 0.0).astype(BF16)
        patch_out[rows, :] = dot_nn(chosen, fgrad[...]).astype(BF16)


def body(n_p, n_z, sp, tp, positions, weight, pp, qp):
    patches, dim = sp.shape
    tokens = positions.shape[0]
    protos = pp.shape[0]
    share = tokens // GROUP
    octets = n_p // GROUP
    vmem = pltpu.VMEM
    dma = pltpu.SemaphoreType.DMA
    one = max(octets - 1, 1)
    scratch = [
        vmem((tokens, patches), BF16),
        vmem((n_z, tokens, 2 * dim), BF16),
        vmem((tokens, dim), F32),
        vmem((tokens, LANES), F32),
        vmem((protos, dim), BF16),
        vmem((protos, dim), BF16),
        vmem((tokens, protos), F32),
        vmem((tokens, protos), F32),
        vmem((tokens, LANES), F32),
        vmem((tokens, LANES), F32),
        vmem((tokens, LANES), F32),
        vmem((tokens, LANES), F32),
        vmem((protos, LANES), F32),
        vmem((1, protos), F32),
        vmem((ITERS, n_p, 2, tokens), F32),
        vmem((ITERS, n_z, 1, protos), F32),
        vmem((n_z, 2, tokens), F32),
        vmem((tokens, dim), F32),
        vmem((GROUP - 1, share, dim), F32),
        vmem((octets, share, dim), F32),
        vmem((tokens, dim), BF16),
        dma((ITERS, n_p - 1)), dma((ITERS, n_p - 1)),
        dma((ITERS, n_z - 1)), dma((ITERS, n_z - 1)),
        dma((n_z - 1,)), dma((n_z - 1,)),
        dma((n_z - 1,)), dma((n_z - 1,)),
        dma((n_z - 1, GROUP // 2 - 1)), dma((n_z - 1, GROUP // 2 - 1)),
        dma((n_z - 1,)), dma((n_z - 1,)),
        dma((GROUP - 1,)), dma((GROUP - 1,)),
        dma((one,)), dma((one,)),
        dma((GROUP - 1,)), dma((GROUP - 1,)),
    ]
    spec = pl.BlockSpec(memory_space=pltpu.VMEM)
    return pl.pallas_call(
        functools.partial(kernel, n_p, n_z),
        out_shape=(
            jax.ShapeDtypeStruct((patches, dim), BF16),
            jax.ShapeDtypeStruct((protos, dim), BF16),
        ),
        in_specs=[spec] * 6,
        out_specs=(spec, spec),
        scratch_shapes=scratch,
        compiler_params=pltpu.CompilerParams(
            collective_id=0, has_side_effects=True, vmem_limit_bytes=58 * 1024 * 1024
        ),
    )(sp, tp, positions.reshape(1, tokens), weight.reshape(1, tokens), pp, qp)


def solution(mesh):
    return jax.shard_map(
        functools.partial(body, mesh.shape["proto"], mesh.shape["batch"]),
        mesh=mesh,
        in_specs=(
            P("batch", None),
            P("batch", None),
            P("batch"),
            P("batch"),
            P("proto", None),
            P("proto", None),
        ),
        out_specs=(P("batch", None), P("proto", None)),
        check_vma=False,
    )
```

```python
import functools
import math

import jax
import jax.numpy as jnp
from jax import lax
from jax.experimental import pallas as pl
from jax.experimental.pallas import tpu as pltpu
from jax.sharding import PartitionSpec as P

ITERS = 3
TEMP_TEACHER = 0.07
TEMP_STUDENT = 0.1
LENGTH_FLOOR = 1e-12
LOG2E = math.log2(math.e)
TEACHER_RATE = LOG2E / TEMP_TEACHER
STUDENT_RATE = LOG2E / TEMP_STUDENT
GROUP = 8
TILE = 256
WIDE = 512
LANES = 128
MESH = pl.DeviceIdType.MESH
F32 = jnp.float32
BF16 = jnp.bfloat16


def dot_nt(a, b):
    return lax.dot_general(a, b, (((1,), (1,)), ((), ())), preferred_element_type=F32)


def dot_nn(a, b):
    return jnp.dot(a, b, preferred_element_type=F32)


def row_norm(values):
    return jnp.sqrt(jnp.sum(values * values, axis=1, keepdims=True) + LENGTH_FLOOR)


def as_columns(row):
    return jnp.transpose(jnp.broadcast_to(row, (LANES, row.shape[1])))


def kernel(
    n_p, n_z,
    sp, tp, pos, weight, pp, qp,
    patch_out, proto_out,
    hot, hot_t, tok_s, tok_t, s_unit, s_norm, ph, qh, e_ref, s_ref, acc_ref, acc2_ref,
    rb_ref, ab_ref, cb_ref, crow_ref,
    row_buf, col_buf, fac_buf, feat, pair_buf, rs_buf, rs2_buf, fgrad,
    row_send, row_recv, col_send, col_recv, fac_send, fac_recv,
    t1_send, t1_recv, t2_send, t2_recv, t3_send, t3_recv,
    pair_send, pair_recv, rs_send, rs_recv, rs2_send, rs2_recv, ag_send, ag_recv,
):
    tokens = tok_s.shape[1]
    patches, dim = sp.shape
    protos = pp.shape[0]
    share = tokens // GROUP
    octets = n_p // GROUP
    me_p = lax.axis_index("proto")
    me_z = lax.axis_index("batch")
    octet = me_p // GROUP
    g = me_p % GROUP

    def rows_of(member):
        return pl.multiple_of(((member % 2) * (GROUP // 2) + member // 2) * share, 16)

    barrier = pltpu.get_barrier_semaphore()
    for j in range(1, n_p):
        pl.semaphore_signal(barrier, inc=1, device_id=((me_p + j) % n_p, me_z), device_id_type=MESH)
    for j in range(1, n_z):
        pl.semaphore_signal(barrier, inc=1, device_id=(me_p, (me_z + j) % n_z), device_id_type=MESH)

    def remote(src, dst, send, recv, p, z):
        return pltpu.make_async_remote_copy(
            src_ref=src, dst_ref=dst, send_sem=send, recv_sem=recv,
            device_id=(p, z), device_id_type=MESH,
        )

    def row_copies(it):
        mine = row_buf.at[it, me_p]
        return [
            remote(mine, mine, row_send.at[it, j - 1], row_recv.at[it, j - 1], (me_p + j) % n_p, me_z)
            for j in range(1, n_p)
        ]

    def col_copies(it):
        mine = col_buf.at[it, me_z]
        return [
            remote(mine, mine, col_send.at[it, j - 1], col_recv.at[it, j - 1], me_p, (me_z + j) % n_z)
            for j in range(1, n_z)
        ]

    def start(copies):
        for copy in copies:
            copy.start()

    def wait(copies):
        for copy in copies:
            copy.wait()

    local = pos[...].reshape(1, tokens) - me_z * patches
    local_col = as_columns(local.astype(F32))
    lane = lax.broadcasted_iota(jnp.int32, (tokens, LANES), 1).astype(F32)
    for t in range(patches // LANES):
        hot[:, t * LANES:(t + 1) * LANES] = jnp.where(
            local_col == lane + float(t * LANES), 1.0, 0.0
        ).astype(BF16)

    @pl.loop(0, tokens // LANES, unroll=True)
    def _(i):
        rows = pl.ds(pl.multiple_of(i * LANES, LANES), LANES)
        picked = hot[rows, :]
        student = dot_nn(picked, sp[...])
        norm = row_norm(student)
        unit = student / norm
        s_unit[rows, :] = unit
        s_norm[rows, :] = jnp.broadcast_to(norm, (LANES, LANES))
        teacher = dot_nn(picked, tp[...])
        tok_s[me_z, rows, :] = unit.astype(BF16)
        tok_t[me_z, rows, :] = (teacher / row_norm(teacher)).astype(BF16)

    @pl.loop(0, protos // TILE, unroll=4)
    def _(i):
        rows = pl.ds(pl.multiple_of(i * TILE, TILE), TILE)
        values = qp[rows, :].astype(F32)
        half = (values / row_norm(values)).astype(BF16)
        qh[rows, :] = half
        exps = jnp.exp2(dot_nt(tok_t[me_z], half) * TEACHER_RATE)
        e_ref[:, rows] = exps
        col_buf[0, me_z, :, rows] = jnp.sum(exps, axis=0, keepdims=True)

    pl.semaphore_wait(barrier, n_p + n_z - 2)
    copies = col_copies(0)
    start(copies)

    acc2_ref[...] = jnp.zeros_like(acc2_ref)

    @pl.loop(0, protos // TILE, unroll=4)
    def _(i):
        rows = pl.ds(pl.multiple_of(i * TILE, TILE), TILE)
        values = pp[rows, :].astype(F32)
        half = (values / row_norm(values)).astype(BF16)
        ph[rows, :] = half
        exps = jnp.exp2(dot_nt(tok_s[me_z], half) * STUDENT_RATE)
        s_ref[:, rows] = exps
        acc2_ref[...] += exps[:, 0:LANES] + exps[:, LANES:2 * LANES]

    def lane_sums(ref):
        return jnp.sum(jnp.transpose(ref[...]), axis=0, keepdims=True)

    other = me_p + 1 - 2 * (me_p % 2)
    half_rows = pl.ds(pl.multiple_of((g % 2) * (tokens // 2), 16), tokens // 2)
    t1, t2, t3 = ([], []), ([], []), ([], [])
    for h, tok in enumerate((tok_t, tok_s)):
        for j in range(1, n_z):
            block = tok.at[me_z, pl.ds(rows_of(g), share), :]
            t1[h].append(remote(
                block, block, t1_send.at[h, j - 1], t1_recv.at[h, j - 1], me_p, (me_z + j) % n_z,
            ))
            source = (me_z + n_z - j) % n_z
            block = tok.at[source, pl.ds(rows_of(g), share), :]
            for k in range(1, GROUP // 2):
                t2[h].append(remote(
                    block, block, t2_send.at[h, j - 1, k - 1], t2_recv.at[h, j - 1, k - 1],
                    octet * GROUP + (g + 2 * k) % GROUP, me_z,
                ))
            block = tok.at[source, half_rows, :]
            t3[h].append(remote(block, block, t3_send.at[h, j - 1], t3_recv.at[h, j - 1], other, me_z))

    row_scale = jnp.ones((1, tokens), F32)
    student_total = None
    for it in range(ITERS):
        if it > 0:
            def col_step(i, carry):
                rows = pl.ds(pl.multiple_of(i * 32, 32), 32)
                scale = rb_ref[rows, :]
                out = []
                for t in range(protos // LANES):
                    part = e_ref[rows, t * LANES:(t + 1) * LANES] * scale
                    out.append(carry[t] + jnp.sum(part.reshape(4, 8, LANES), axis=0))
                return tuple(out)
            sums = lax.fori_loop(
                0, tokens // 32, col_step,
                tuple(jnp.zeros((8, LANES), F32) for _ in range(protos // LANES)),
            )
            for t in range(protos // LANES):
                col_buf[it, me_z, :, t * LANES:(t + 1) * LANES] = jnp.sum(sums[t], axis=0, keepdims=True)
            copies = col_copies(it)
            start(copies)
        if it == 1:
            index = lax.broadcasted_iota(jnp.int32, (LANES, tokens), 0)
            for t in range(patches // LANES):
                hot_t[t * LANES:(t + 1) * LANES, :] = jnp.where(
                    index + t * LANES == local, 1.0, 0.0
                ).astype(BF16)
        wait(copies)
        if it < 2:
            start(t1[it])
        total = col_buf[it, 0]
        for q in range(1, n_z):
            total = total + col_buf[it, q]
        crow_ref[...] = 1.0 / total

        @pl.loop(0, tokens // 64, unroll=2)
        def _(i):
            rows = pl.ds(pl.multiple_of(i * 64, 64), 64)
            running = e_ref[rows, 0:LANES] * crow_ref[:, 0:LANES]
            for t in range(1, protos // LANES):
                cols = slice(t * LANES, (t + 1) * LANES)
                running = running + e_ref[rows, cols] * crow_ref[:, cols]
            acc_ref[rows, :] = running

        row_buf[it, me_p, 0:1, :] = lane_sums(acc_ref)
        row_buf[it, me_p, 1:2, :] = lane_sums(acc2_ref)
        copies = row_copies(it)
        start(copies)
        if it == ITERS - 1:
            cb_ref[...] = as_columns(crow_ref[...])
        wait(copies)
        if it == 1:
            wait(t2[0])
            start(t3[0])
        if it < 2:
            wait(t1[it])
            start(t2[it])
        total = row_buf[it, 0]
        for q in range(1, n_p):
            total = total + row_buf[it, q]
        row_scale = row_scale / (row_scale * total[0:1, :])
        student_total = total[1:2, :]
        if it < ITERS - 1:
            rb_ref[...] = as_columns(row_scale)

    gain = weight[...].reshape(1, tokens) / TEMP_STUDENT
    student_gain = gain / student_total
    teacher_gain = gain * row_scale
    fac_buf[me_z, 0:1, :] = student_gain
    fac_buf[me_z, 1:2, :] = teacher_gain
    mine = fac_buf.at[me_z]
    fac = [
        remote(mine, mine, fac_send.at[j - 1], fac_recv.at[j - 1], me_p, (me_z + j) % n_z)
        for j in range(1, n_z)
    ]
    start(fac)
    wait(t2[1])
    start(t3[1])

    rb_ref[...] = as_columns(teacher_gain)
    ab_ref[...] = as_columns(student_gain)

    def feature_rows(first, count):
        rows = pl.ds(pl.multiple_of(first, 16), count)
        a = ab_ref[rows, :]
        b = rb_ref[rows, :]
        parts = []
        for t in range(protos // LANES):
            cols = slice(t * LANES, (t + 1) * LANES)
            parts.append(
                (s_ref[rows, cols] * a - e_ref[rows, cols] * b * crow_ref[:, cols]).astype(BF16)
            )
        feat[rows, :] = dot_nn(jnp.concatenate(parts, axis=1), ph[...])
        return rows

    quarter = tokens // 4
    theirs = ((g + 1) % 2) * (tokens // 2)
    ours = (g % 2) * (tokens // 2)
    pair = []
    for i in range(2):
        rows = feature_rows(theirs + i * quarter, quarter)
        pair.append(remote(
            feat.at[rows, :], pair_buf.at[i], pair_send.at[i], pair_recv.at[i], other, me_z,
        ))
        start(pair[i:])
    for i in range(2):
        feature_rows(ours + i * quarter, quarter)


    def proto_tile(i):
        rows = pl.ds(pl.multiple_of(i * WIDE, WIDE), WIDE)
        p_half = ph[rows, :]
        q_half = qh[rows, :]
        c = jnp.concatenate([cb_ref[rows, :]] * (tokens // LANES), axis=1)

        def block(z, running):
            student = tok_s[z]
            prob = jnp.exp2(dot_nt(p_half, student) * STUDENT_RATE)
            target = jnp.exp2(dot_nt(q_half, tok_t[z]) * TEACHER_RATE)
            coefficient = prob * fac_buf[z, 0:1, :] - target * fac_buf[z, 1:2, :] * c
            return running + dot_nn(coefficient.astype(BF16), student)

        total = jnp.zeros((WIDE, dim), F32)
        if n_z <= 4:
            for z in range(n_z):
                total = block(z, total)
        else:
            total = lax.fori_loop(0, n_z, block, total)
        values = pp[rows, :].astype(F32)
        norm = row_norm(values)
        unit = values / norm
        inner = jnp.sum(total * unit, axis=1, keepdims=True)
        proto_out[rows, :] = ((total - inner * unit) / norm).astype(BF16)

    tiles = protos // WIDE
    wait(pair)
    for i in range(2):
        rows = pl.ds(pl.multiple_of(ours + i * quarter, 16), quarter)
        feat[rows, :] += pair_buf[i]
    rs = []
    for j in range(1, GROUP // 2):
        to = (g + 2 * j) % GROUP
        rs.append(remote(
            feat.at[pl.ds(rows_of(to), share), :], rs_buf.at[j - 1],
            rs_send.at[j - 1], rs_recv.at[j - 1], octet * GROUP + to, me_z,
        ))
    start(rs)
    wait(fac)
    wait(t3[0])
    wait(t3[1])
    early = tiles // 2
    pl.loop(0, early)(proto_tile)

    wait(rs)
    own = pl.ds(rows_of(g), share)
    total = feat[own, :]
    for j in range(1, GROUP // 2):
        total = total + rs_buf[j - 1]
    if octets > 1:
        rs2_buf[octet] = total
        mine2 = rs2_buf.at[octet]
        rs2 = [
            remote(mine2, mine2, rs2_send.at[j - 1], rs2_recv.at[j - 1],
                   ((octet + j) % octets) * GROUP + g, me_z)
            for j in range(1, octets)
        ]
        start(rs2)
        wait(rs2)
        total = rs2_buf[0]
        for q in range(1, octets):
            total = total + rs2_buf[q]
    unit = s_unit[own, :]
    inner = jnp.sum(total * unit, axis=1, keepdims=True)
    norm = jnp.concatenate([s_norm[own, :]] * (dim // LANES), axis=1)
    fgrad[own, :] = ((total - inner * unit) / norm).astype(BF16)
    piece = fgrad.at[own, :]
    ag = [
        remote(piece, piece, ag_send.at[j - 1], ag_recv.at[j - 1],
               octet * GROUP + (g + j) % GROUP, me_z)
        for j in range(1, GROUP)
    ]
    start(ag)

    pl.loop(early, tiles)(proto_tile)

    wait(ag)

    @pl.loop(0, patches // TILE)
    def _(i):
        rows = pl.ds(pl.multiple_of(i * TILE, TILE), TILE)
        patch_out[rows, :] = dot_nn(hot_t[rows, :], fgrad[...]).astype(BF16)


def body(n_p, n_z, sp, tp, positions, weight, pp, qp):
    patches, dim = sp.shape
    tokens = positions.shape[0]
    protos = pp.shape[0]
    share = tokens // GROUP
    octets = n_p // GROUP
    vmem = pltpu.VMEM
    dma = pltpu.SemaphoreType.DMA
    one = max(octets - 1, 1)
    scratch = [
        vmem((tokens, patches), BF16),
        vmem((patches, tokens), BF16),
        vmem((n_z, tokens, dim), BF16),
        vmem((n_z, tokens, dim), BF16),
        vmem((tokens, dim), F32),
        vmem((tokens, LANES), F32),
        vmem((protos, dim), BF16),
        vmem((protos, dim), BF16),
        vmem((tokens, protos), F32),
        vmem((tokens, protos), F32),
        vmem((tokens, LANES), F32),
        vmem((tokens, LANES), F32),
        vmem((tokens, LANES), F32),
        vmem((tokens, LANES), F32),
        vmem((protos, LANES), F32),
        vmem((1, protos), F32),
        vmem((ITERS, n_p, 2, tokens), F32),
        vmem((ITERS, n_z, 1, protos), F32),
        vmem((n_z, 2, tokens), F32),
        vmem((tokens, dim), F32),
        vmem((2, tokens // 4, dim), F32),
        vmem((GROUP // 2 - 1, share, dim), F32),
        vmem((octets, share, dim), F32),
        vmem((tokens, dim), BF16),
        dma((ITERS, n_p - 1)), dma((ITERS, n_p - 1)),
        dma((ITERS, n_z - 1)), dma((ITERS, n_z - 1)),
        dma((n_z - 1,)), dma((n_z - 1,)),
        dma((2, n_z - 1)), dma((2, n_z - 1)),
        dma((2, n_z - 1, GROUP // 2 - 1)), dma((2, n_z - 1, GROUP // 2 - 1)),
        dma((2, n_z - 1)), dma((2, n_z - 1)),
        dma((2,)), dma((2,)),
        dma((GROUP // 2 - 1,)), dma((GROUP // 2 - 1,)),
        dma((one,)), dma((one,)),
        dma((GROUP - 1,)), dma((GROUP - 1,)),
    ]
    spec = pl.BlockSpec(memory_space=pltpu.VMEM)
    return pl.pallas_call(
        functools.partial(kernel, n_p, n_z),
        out_shape=(
            jax.ShapeDtypeStruct((patches, dim), BF16),
            jax.ShapeDtypeStruct((protos, dim), BF16),
        ),
        in_specs=[spec] * 6,
        out_specs=(spec, spec),
        scratch_shapes=scratch,
        compiler_params=pltpu.CompilerParams(
            collective_id=0, has_side_effects=True, vmem_limit_bytes=58 * 1024 * 1024
        ),
    )(sp, tp, positions, weight, pp, qp)


def solution(mesh):
    return jax.shard_map(
        functools.partial(body, mesh.shape["proto"], mesh.shape["batch"]),
        mesh=mesh,
        in_specs=(
            P("batch", None),
            P("batch", None),
            P("batch"),
            P("batch"),
            P("proto", None),
            P("proto", None),
        ),
        out_specs=(P("batch", None), P("proto", None)),
        check_vma=False,
    )
```

```python
import functools
import math

import jax
import jax.numpy as jnp
from jax import lax
from jax.experimental import pallas as pl
from jax.experimental.pallas import tpu as pltpu
from jax.sharding import PartitionSpec as P

ITERS = 3
TEMP_TEACHER = 0.07
TEMP_STUDENT = 0.1
LENGTH_FLOOR = 1e-12
LOG2E = math.log2(math.e)
TEACHER_RATE = LOG2E / TEMP_TEACHER
STUDENT_RATE = LOG2E / TEMP_STUDENT
GROUP = 8
TILE = 256
WIDE = 1024
CHUNK = 512
LANES = 128
MESH = pl.DeviceIdType.MESH
F32 = jnp.float32
BF16 = jnp.bfloat16


def dot_nt(a, b):
    return lax.dot_general(a, b, (((1,), (1,)), ((), ())), preferred_element_type=F32)


def dot_nn(a, b):
    return jnp.dot(a, b, preferred_element_type=F32)


def row_norm(values):
    return jnp.sqrt(jnp.sum(values * values, axis=1, keepdims=True) + LENGTH_FLOOR)


def as_columns(row):
    return jnp.transpose(jnp.broadcast_to(row, (LANES, row.shape[1])))


def kernel(
    n_p, n_z,
    sp, tp, pos, weight, pp_in, qp_in,
    patch_out, proto_out,
    pp, qp, load_sem, hot, hot_t, tok_s, tok_t, fac_flat, s_unit, s_norm, ph, qh, e_ref, s_ref, acc_ref, acc2_ref,
    rb_ref, ab_ref, cb_ref, crow_ref,
    row_buf, col_buf, fac_buf, feat, pair_buf, rs_buf, rs2_buf, fgrad,
    row_send, row_recv, col_send, col_recv, fac_send, fac_recv,
    t1_send, t1_recv, t2_send, t2_recv, t3_send, t3_recv,
    pair_send, pair_recv, rs_send, rs_recv, rs2_send, rs2_recv, ag_send, ag_recv,
):
    tokens = pos.shape[0]
    patches, dim = sp.shape
    protos = pp.shape[0]
    share = tokens // GROUP
    octets = n_p // GROUP
    me_p = lax.axis_index("proto")
    me_z = lax.axis_index("batch")
    octet = me_p // GROUP
    g = me_p % GROUP

    def block_rows(z, first, count):
        return pl.ds(pl.multiple_of(z * tokens + first, 16), count)

    def rows_of(member):
        return pl.multiple_of(((member % 2) * (GROUP // 2) + member // 2) * share, 16)

    loads = [
        pltpu.make_async_copy(qp_in, qp, load_sem.at[0]),
        pltpu.make_async_copy(pp_in, pp, load_sem.at[1]),
    ]
    for load in loads:
        load.start()
    barrier = pltpu.get_barrier_semaphore()
    for j in range(1, n_p):
        pl.semaphore_signal(barrier, inc=1, device_id=((me_p + j) % n_p, me_z), device_id_type=MESH)
    for j in range(1, n_z):
        pl.semaphore_signal(barrier, inc=1, device_id=(me_p, (me_z + j) % n_z), device_id_type=MESH)

    def remote(src, dst, send, recv, p, z):
        return pltpu.make_async_remote_copy(
            src_ref=src, dst_ref=dst, send_sem=send, recv_sem=recv,
            device_id=(p, z), device_id_type=MESH,
        )

    def row_copies(it):
        mine = row_buf.at[it, me_p]
        return [
            remote(mine, mine, row_send.at[it, j - 1], row_recv.at[it, j - 1], (me_p + j) % n_p, me_z)
            for j in range(1, n_p)
        ]

    def col_copies(it):
        mine = col_buf.at[it, me_z]
        return [
            remote(mine, mine, col_send.at[it, j - 1], col_recv.at[it, j - 1], me_p, (me_z + j) % n_z)
            for j in range(1, n_z)
        ]

    def start(copies):
        for copy in copies:
            copy.start()

    pending = []

    def wait(copies):
        for copy in copies:
            copy.wait_recv()
        pending.extend(copies)

    local = pos[...].reshape(1, tokens) - me_z * patches
    local_col = as_columns(local.astype(F32))
    lane = lax.broadcasted_iota(jnp.int32, (tokens, LANES), 1).astype(F32)
    for t in range(patches // LANES):
        hot[:, t * LANES:(t + 1) * LANES] = jnp.where(
            local_col == lane + float(t * LANES), 1.0, 0.0
        ).astype(BF16)

    @pl.loop(0, tokens // LANES, unroll=True)
    def _(i):
        rows = pl.ds(pl.multiple_of(i * LANES, LANES), LANES)
        picked = hot[rows, :]
        student = dot_nn(picked, sp[...])
        norm = row_norm(student)
        unit = student / norm
        s_unit[rows, :] = unit
        s_norm[rows, :] = jnp.broadcast_to(norm, (LANES, LANES))
        teacher = dot_nn(picked, tp[...])
        tok_s[block_rows(me_z, i * LANES, LANES), :] = unit.astype(BF16)
        tok_t[block_rows(me_z, i * LANES, LANES), :] = (teacher / row_norm(teacher)).astype(BF16)

    loads[0].wait()

    @pl.loop(0, protos // TILE, unroll=4)
    def _(i):
        rows = pl.ds(pl.multiple_of(i * TILE, TILE), TILE)
        values = qp[rows, :].astype(F32)
        half = (values / row_norm(values)).astype(BF16)
        qh[rows, :] = half
        exps = jnp.exp2(dot_nt(tok_t[block_rows(me_z, 0, tokens), :], half) * TEACHER_RATE)
        e_ref[:, rows] = exps
        col_buf[0, me_z, :, rows] = jnp.sum(exps, axis=0, keepdims=True)

    pl.semaphore_wait(barrier, n_p + n_z - 2)
    copies = col_copies(0)
    start(copies)

    acc2_ref[...] = jnp.zeros_like(acc2_ref)
    loads[1].wait()

    @pl.loop(0, protos // TILE, unroll=4)
    def _(i):
        rows = pl.ds(pl.multiple_of(i * TILE, TILE), TILE)
        values = pp[rows, :].astype(F32)
        half = (values / row_norm(values)).astype(BF16)
        ph[rows, :] = half
        exps = jnp.exp2(dot_nt(tok_s[block_rows(me_z, 0, tokens), :], half) * STUDENT_RATE)
        s_ref[:, rows] = exps
        acc2_ref[...] += exps[:, 0:LANES] + exps[:, LANES:2 * LANES]

    def lane_sums(ref):
        return jnp.sum(jnp.transpose(ref[...]), axis=0, keepdims=True)

    other = me_p + 1 - 2 * (me_p % 2)
    t1, t2, t3 = ([], []), ([], []), ([], [])
    for h, tok in enumerate((tok_t, tok_s)):
        for j in range(1, n_z):
            block = tok.at[block_rows(me_z, rows_of(g), share), :]
            t1[h].append(remote(
                block, block, t1_send.at[h, j - 1], t1_recv.at[h, j - 1], me_p, (me_z + j) % n_z,
            ))
            source = (me_z + n_z - j) % n_z
            block = tok.at[block_rows(source, rows_of(g), share), :]
            for k in range(1, GROUP // 2):
                t2[h].append(remote(
                    block, block, t2_send.at[h, j - 1, k - 1], t2_recv.at[h, j - 1, k - 1],
                    octet * GROUP + (g + 2 * k) % GROUP, me_z,
                ))
            block = tok.at[block_rows(source, (g % 2) * (tokens // 2), tokens // 2), :]
            t3[h].append(remote(block, block, t3_send.at[h, j - 1], t3_recv.at[h, j - 1], other, me_z))

    row_scale = jnp.ones((1, tokens), F32)
    student_total = None
    for it in range(ITERS):
        if it > 0:
            def col_step(i, carry):
                rows = pl.ds(pl.multiple_of(i * 32, 32), 32)
                scale = rb_ref[rows, :]
                out = []
                for t in range(protos // LANES):
                    part = e_ref[rows, t * LANES:(t + 1) * LANES] * scale
                    out.append(carry[t] + jnp.sum(part.reshape(4, 8, LANES), axis=0))
                return tuple(out)
            sums = lax.fori_loop(
                0, tokens // 32, col_step,
                tuple(jnp.zeros((8, LANES), F32) for _ in range(protos // LANES)),
            )
            for t in range(protos // LANES):
                col_buf[it, me_z, :, t * LANES:(t + 1) * LANES] = jnp.sum(sums[t], axis=0, keepdims=True)
            copies = col_copies(it)
            start(copies)
        if it == 1:
            index = lax.broadcasted_iota(jnp.int32, (LANES, tokens), 0)
            for t in range(patches // LANES):
                hot_t[t * LANES:(t + 1) * LANES, :] = jnp.where(
                    index + t * LANES == local, 1.0, 0.0
                ).astype(BF16)
        wait(copies)
        if it < 2:
            start(t1[it])
        total = col_buf[it, 0]
        for q in range(1, n_z):
            total = total + col_buf[it, q]
        crow_ref[...] = 1.0 / total

        @pl.loop(0, tokens // 64, unroll=2)
        def _(i):
            rows = pl.ds(pl.multiple_of(i * 64, 64), 64)
            running = e_ref[rows, 0:LANES] * crow_ref[:, 0:LANES]
            for t in range(1, protos // LANES):
                cols = slice(t * LANES, (t + 1) * LANES)
                running = running + e_ref[rows, cols] * crow_ref[:, cols]
            acc_ref[rows, :] = running

        row_buf[it, me_p, 0:1, :] = lane_sums(acc_ref)
        row_buf[it, me_p, 1:2, :] = lane_sums(acc2_ref)
        copies = row_copies(it)
        start(copies)
        if it == ITERS - 1:
            cb_ref[...] = as_columns(crow_ref[...])
        wait(copies)
        if it == 1:
            wait(t2[0])
            start(t3[0])
        if it < 2:
            wait(t1[it])
            start(t2[it])
        total = row_buf[it, 0]
        for q in range(1, n_p):
            total = total + row_buf[it, q]
        row_scale = row_scale / (row_scale * total[0:1, :])
        student_total = total[1:2, :]
        if it < ITERS - 1:
            rb_ref[...] = as_columns(row_scale)

    gain = weight[...].reshape(1, tokens) / TEMP_STUDENT
    student_gain = gain / student_total
    teacher_gain = gain * row_scale
    fac_buf[me_z, 0:1, :] = student_gain
    fac_buf[me_z, 1:2, :] = teacher_gain
    mine = fac_buf.at[me_z]
    fac = [
        remote(mine, mine, fac_send.at[j - 1], fac_recv.at[j - 1], me_p, (me_z + j) % n_z)
        for j in range(1, n_z)
    ]
    start(fac)
    wait(t2[1])
    start(t3[1])

    rb_ref[...] = as_columns(teacher_gain)
    ab_ref[...] = as_columns(student_gain)

    def feature_rows(first, count):
        rows = pl.ds(pl.multiple_of(first, 16), count)
        a = ab_ref[rows, :]
        b = rb_ref[rows, :]
        parts = []
        for t in range(protos // LANES):
            cols = slice(t * LANES, (t + 1) * LANES)
            parts.append(
                (s_ref[rows, cols] * a - e_ref[rows, cols] * b * crow_ref[:, cols]).astype(BF16)
            )
        feat[rows, :] = dot_nn(jnp.concatenate(parts, axis=1), ph[...])
        return rows

    quarter = tokens // 4
    theirs = ((g + 1) % 2) * (tokens // 2)
    ours = (g % 2) * (tokens // 2)
    pair = []
    for i in range(2):
        rows = feature_rows(theirs + i * quarter, quarter)
        pair.append(remote(
            feat.at[rows, :], pair_buf.at[i], pair_send.at[i], pair_recv.at[i], other, me_z,
        ))
        start(pair[i:])
    for i in range(2):
        feature_rows(ours + i * quarter, quarter)


    def proto_tile(i):
        rows = pl.ds(pl.multiple_of(i * WIDE, WIDE), WIDE)
        p_half = ph[rows, :]
        q_half = qh[rows, :]
        c = jnp.concatenate([cb_ref[rows, :]] * (CHUNK // LANES), axis=1)

        def block(k, running):
            part = pl.ds(pl.multiple_of(k * CHUNK, CHUNK), CHUNK)
            student = tok_s[part, :]
            prob = jnp.exp2(dot_nt(p_half, student) * STUDENT_RATE)
            target = jnp.exp2(dot_nt(q_half, tok_t[part, :]) * TEACHER_RATE)
            coefficient = prob * fac_flat[0:1, part] - target * fac_flat[1:2, part] * c
            return running + dot_nn(coefficient.astype(BF16), student)

        total = jnp.zeros((WIDE, dim), F32)
        chunks = n_z * tokens // CHUNK
        if chunks <= 5:
            for k in range(chunks):
                total = block(k, total)
        else:
            total = lax.fori_loop(0, chunks, block, total)
        values = pp[rows, :].astype(F32)
        norm = row_norm(values)
        unit = values / norm
        inner = jnp.sum(total * unit, axis=1, keepdims=True)
        proto_out[rows, :] = ((total - inner * unit) / norm).astype(BF16)

    tiles = protos // WIDE
    wait(pair)
    for i in range(2):
        rows = pl.ds(pl.multiple_of(ours + i * quarter, 16), quarter)
        feat[rows, :] += pair_buf[i]
    rs = []
    for j in range(1, GROUP // 2):
        to = (g + 2 * j) % GROUP
        rs.append(remote(
            feat.at[pl.ds(rows_of(to), share), :], rs_buf.at[j - 1],
            rs_send.at[j - 1], rs_recv.at[j - 1], octet * GROUP + to, me_z,
        ))
    start(rs)
    wait(fac)
    wait(t3[0])
    wait(t3[1])
    for z in range(n_z):
        fac_flat[:, z * tokens:(z + 1) * tokens] = fac_buf[z]
    early = tiles // 2
    pl.loop(0, early)(proto_tile)

    wait(rs)
    own = pl.ds(rows_of(g), share)
    total = feat[own, :]
    for j in range(1, GROUP // 2):
        total = total + rs_buf[j - 1]
    if octets > 1:
        rs2_buf[octet] = total
        mine2 = rs2_buf.at[octet]
        rs2 = [
            remote(mine2, mine2, rs2_send.at[j - 1], rs2_recv.at[j - 1],
                   ((octet + j) % octets) * GROUP + g, me_z)
            for j in range(1, octets)
        ]
        start(rs2)
        wait(rs2)
        total = rs2_buf[0]
        for q in range(1, octets):
            total = total + rs2_buf[q]
    unit = s_unit[own, :]
    inner = jnp.sum(total * unit, axis=1, keepdims=True)
    norm = jnp.concatenate([s_norm[own, :]] * (dim // LANES), axis=1)
    fgrad[own, :] = ((total - inner * unit) / norm).astype(BF16)
    piece = fgrad.at[own, :]
    ag = [
        remote(piece, piece, ag_send.at[j - 1], ag_recv.at[j - 1],
               octet * GROUP + (g + j) % GROUP, me_z)
        for j in range(1, GROUP)
    ]
    start(ag)

    pl.loop(early, tiles)(proto_tile)

    wait(ag)
    for copy in pending:
        copy.wait_send()

    @pl.loop(0, patches // TILE)
    def _(i):
        rows = pl.ds(pl.multiple_of(i * TILE, TILE), TILE)
        patch_out[rows, :] = dot_nn(hot_t[rows, :], fgrad[...]).astype(BF16)


def body(n_p, n_z, sp, tp, positions, weight, pp, qp):
    patches, dim = sp.shape
    tokens = positions.shape[0]
    protos = pp.shape[0]
    share = tokens // GROUP
    octets = n_p // GROUP
    vmem = pltpu.VMEM
    dma = pltpu.SemaphoreType.DMA
    one = max(octets - 1, 1)
    scratch = [
        vmem((protos, dim), BF16),
        vmem((protos, dim), BF16),
        dma((2,)),
        vmem((tokens, patches), BF16),
        vmem((patches, tokens), BF16),
        vmem((n_z * tokens, dim), BF16),
        vmem((n_z * tokens, dim), BF16),
        vmem((2, n_z * tokens), F32),
        vmem((tokens, dim), F32),
        vmem((tokens, LANES), F32),
        vmem((protos, dim), BF16),
        vmem((protos, dim), BF16),
        vmem((tokens, protos), F32),
        vmem((tokens, protos), F32),
        vmem((tokens, LANES), F32),
        vmem((tokens, LANES), F32),
        vmem((tokens, LANES), F32),
        vmem((tokens, LANES), F32),
        vmem((protos, LANES), F32),
        vmem((1, protos), F32),
        vmem((ITERS, n_p, 2, tokens), F32),
        vmem((ITERS, n_z, 1, protos), F32),
        vmem((n_z, 2, tokens), F32),
        vmem((tokens, dim), F32),
        vmem((2, tokens // 4, dim), F32),
        vmem((GROUP // 2 - 1, share, dim), F32),
        vmem((octets, share, dim), F32),
        vmem((tokens, dim), BF16),
        dma((ITERS, n_p - 1)), dma((ITERS, n_p - 1)),
        dma((ITERS, n_z - 1)), dma((ITERS, n_z - 1)),
        dma((n_z - 1,)), dma((n_z - 1,)),
        dma((2, n_z - 1)), dma((2, n_z - 1)),
        dma((2, n_z - 1, GROUP // 2 - 1)), dma((2, n_z - 1, GROUP // 2 - 1)),
        dma((2, n_z - 1)), dma((2, n_z - 1)),
        dma((2,)), dma((2,)),
        dma((GROUP // 2 - 1,)), dma((GROUP // 2 - 1,)),
        dma((one,)), dma((one,)),
        dma((GROUP - 1,)), dma((GROUP - 1,)),
    ]
    spec = pl.BlockSpec(memory_space=pltpu.VMEM)
    return pl.pallas_call(
        functools.partial(kernel, n_p, n_z),
        out_shape=(
            jax.ShapeDtypeStruct((patches, dim), BF16),
            jax.ShapeDtypeStruct((protos, dim), BF16),
        ),
        in_specs=[spec] * 4 + [pl.BlockSpec(memory_space=pl.ANY)] * 2,
        out_specs=(spec, spec),
        scratch_shapes=scratch,
        compiler_params=pltpu.CompilerParams(
            collective_id=0, has_side_effects=True, vmem_limit_bytes=58 * 1024 * 1024
        ),
    )(sp, tp, positions, weight, pp, qp)


def solution(mesh):
    return jax.shard_map(
        functools.partial(body, mesh.shape["proto"], mesh.shape["batch"]),
        mesh=mesh,
        in_specs=(
            P("batch", None),
            P("batch", None),
            P("batch"),
            P("batch"),
            P("proto", None),
            P("proto", None),
        ),
        out_specs=(P("batch", None), P("proto", None)),
        check_vma=False,
    )
```

```python
import functools
import math

import jax
import jax.numpy as jnp
from jax import lax
from jax.experimental import pallas as pl
from jax.experimental.pallas import tpu as pltpu
from jax.sharding import PartitionSpec as P

ITERS = 3
TEMP_TEACHER = 0.07
TEMP_STUDENT = 0.1
LENGTH_FLOOR = 1e-12
LOG2E = math.log2(math.e)
TEACHER_RATE = LOG2E / TEMP_TEACHER
STUDENT_RATE = LOG2E / TEMP_STUDENT
GROUP = 8
TILE = 256
WIDE = 1024
CHUNK = 512
LANES = 128
MESH = pl.DeviceIdType.MESH
F32 = jnp.float32
BF16 = jnp.bfloat16


def dot_nt(a, b):
    return lax.dot_general(a, b, (((1,), (1,)), ((), ())), preferred_element_type=F32)


def dot_nn(a, b):
    return jnp.dot(a, b, preferred_element_type=F32)


def row_norm(values):
    return jnp.sqrt(jnp.sum(values * values, axis=1, keepdims=True) + LENGTH_FLOOR)


def as_columns(row):
    return jnp.transpose(jnp.broadcast_to(row, (LANES, row.shape[1])))


def kernel(
    n_p, n_z,
    sp, tp, pos, weight, pp_in, qp_in,
    patch_out, proto_out,
    pp, qp, load_sem, hot, hot_t, tok_s, tok_t, fac_flat, s_unit, s_norm, ph, qh, e_ref, s_ref, acc_ref, acc2_ref,
    rb_ref, ab_ref, cb_ref, crow_ref,
    row_buf, col_buf, fac_buf, feat, pair_buf, rs_buf, rs2_buf, fgrad,
    row_send, row_recv, col_send, col_recv, fac_send, fac_recv,
    t1_send, t1_recv, t2_send, t2_recv, t3_send, t3_recv,
    pair_send, pair_recv, rs_send, rs_recv, rs2_send, rs2_recv, ag_send, ag_recv,
):
    tokens = pos.shape[0]
    patches, dim = sp.shape
    protos = pp.shape[0]
    share = tokens // GROUP
    octets = n_p // GROUP
    me_p = lax.axis_index("proto")
    me_z = lax.axis_index("batch")
    octet = me_p // GROUP
    g = me_p % GROUP

    def block_rows(z, first, count):
        return pl.ds(pl.multiple_of(z * tokens + first, 16), count)

    def rows_of(member):
        return pl.multiple_of(((member % 2) * (GROUP // 2) + member // 2) * share, 16)

    loads = [
        pltpu.make_async_copy(qp_in, qp, load_sem.at[0]),
        pltpu.make_async_copy(pp_in, pp, load_sem.at[1]),
    ]
    for load in loads:
        load.start()
    barrier = pltpu.get_barrier_semaphore()
    for j in range(1, n_p):
        pl.semaphore_signal(barrier, inc=1, device_id=((me_p + j) % n_p, me_z), device_id_type=MESH)
    for j in range(1, n_z):
        pl.semaphore_signal(barrier, inc=1, device_id=(me_p, (me_z + j) % n_z), device_id_type=MESH)

    def remote(src, dst, send, recv, p, z):
        return pltpu.make_async_remote_copy(
            src_ref=src, dst_ref=dst, send_sem=send, recv_sem=recv,
            device_id=(p, z), device_id_type=MESH,
        )

    def row_copies(it):
        mine = row_buf.at[it, me_p]
        return [
            remote(mine, mine, row_send.at[it, j - 1], row_recv.at[it, j - 1], (me_p + j) % n_p, me_z)
            for j in range(1, n_p)
        ]

    def col_copies(it):
        mine = col_buf.at[it, me_z]
        return [
            remote(mine, mine, col_send.at[it, j - 1], col_recv.at[it, j - 1], me_p, (me_z + j) % n_z)
            for j in range(1, n_z)
        ]

    def start(copies):
        for copy in copies:
            copy.start()

    pending = []

    def wait(copies):
        for copy in copies:
            copy.wait_recv()
        pending.extend(copies)

    local = pos[...].reshape(1, tokens) - me_z * patches
    local_col = as_columns(local.astype(F32))
    lane = lax.broadcasted_iota(jnp.int32, (tokens, LANES), 1).astype(F32)
    for t in range(patches // LANES):
        hot[:, t * LANES:(t + 1) * LANES] = jnp.where(
            local_col == lane + float(t * LANES), 1.0, 0.0
        ).astype(BF16)

    @pl.loop(0, tokens // LANES, unroll=True)
    def _(i):
        rows = pl.ds(pl.multiple_of(i * LANES, LANES), LANES)
        picked = hot[rows, :]
        student = dot_nn(picked, sp[...])
        norm = row_norm(student)
        unit = student / norm
        s_unit[rows, :] = unit
        s_norm[rows, :] = jnp.broadcast_to(norm, (LANES, LANES))
        teacher = dot_nn(picked, tp[...])
        tok_s[block_rows(me_z, i * LANES, LANES), :] = unit.astype(BF16)
        tok_t[block_rows(me_z, i * LANES, LANES), :] = (teacher / row_norm(teacher)).astype(BF16)

    loads[0].wait()

    @pl.loop(0, protos // TILE, unroll=4)
    def _(i):
        rows = pl.ds(pl.multiple_of(i * TILE, TILE), TILE)
        values = qp[rows, :].astype(F32)
        half = (values / row_norm(values)).astype(BF16)
        qh[rows, :] = half
        exps = jnp.exp2(dot_nt(tok_t[block_rows(me_z, 0, tokens), :], half) * TEACHER_RATE)
        e_ref[:, rows] = exps
        col_buf[0, me_z, :, rows] = jnp.sum(exps, axis=0, keepdims=True)

    pl.semaphore_wait(barrier, n_p + n_z - 2)
    copies = col_copies(0)
    start(copies)

    acc2_ref[...] = jnp.zeros_like(acc2_ref)
    loads[1].wait()

    @pl.loop(0, protos // TILE, unroll=4)
    def _(i):
        rows = pl.ds(pl.multiple_of(i * TILE, TILE), TILE)
        values = pp[rows, :].astype(F32)
        half = (values / row_norm(values)).astype(BF16)
        ph[rows, :] = half
        exps = jnp.exp2(dot_nt(tok_s[block_rows(me_z, 0, tokens), :], half) * STUDENT_RATE)
        s_ref[:, rows] = exps
        acc2_ref[...] += exps[:, 0:LANES] + exps[:, LANES:2 * LANES]

    def lane_sums(ref):
        return jnp.sum(jnp.transpose(ref[...]), axis=0, keepdims=True)

    other = me_p + 1 - 2 * (me_p % 2)
    t1, t2, t3 = ([], []), ([], []), ([], [])
    for h, tok in enumerate((tok_t, tok_s)):
        for j in range(1, n_z):
            block = tok.at[block_rows(me_z, rows_of(g), share), :]
            t1[h].append(remote(
                block, block, t1_send.at[h, j - 1], t1_recv.at[h, j - 1], me_p, (me_z + j) % n_z,
            ))
            source = (me_z + n_z - j) % n_z
            block = tok.at[block_rows(source, rows_of(g), share), :]
            for k in range(1, GROUP // 2):
                t2[h].append(remote(
                    block, block, t2_send.at[h, j - 1, k - 1], t2_recv.at[h, j - 1, k - 1],
                    octet * GROUP + (g + 2 * k) % GROUP, me_z,
                ))
            block = tok.at[block_rows(source, (g % 2) * (tokens // 2), tokens // 2), :]
            t3[h].append(remote(block, block, t3_send.at[h, j - 1], t3_recv.at[h, j - 1], other, me_z))

    row_scale = jnp.ones((1, tokens), F32)
    student_total = None
    student_row = lane_sums(acc2_ref)
    for it in range(ITERS):
        if it > 0:
            def col_step(i, carry):
                rows = pl.ds(pl.multiple_of(i * 32, 32), 32)
                scale = rb_ref[rows, :]
                out = []
                for t in range(protos // LANES):
                    part = e_ref[rows, t * LANES:(t + 1) * LANES] * scale
                    out.append(carry[t] + jnp.sum(part.reshape(4, 8, LANES), axis=0))
                return tuple(out)
            sums = lax.fori_loop(
                0, tokens // 32, col_step,
                tuple(jnp.zeros((8, LANES), F32) for _ in range(protos // LANES)),
                unroll=2,
            )
            for t in range(protos // LANES):
                col_buf[it, me_z, :, t * LANES:(t + 1) * LANES] = jnp.sum(sums[t], axis=0, keepdims=True)
            copies = col_copies(it)
            start(copies)
        if it == 1:
            index = lax.broadcasted_iota(jnp.int32, (LANES, tokens), 0)
            for t in range(patches // LANES):
                hot_t[t * LANES:(t + 1) * LANES, :] = jnp.where(
                    index + t * LANES == local, 1.0, 0.0
                ).astype(BF16)
        wait(copies)
        if it < 2:
            start(t1[it])
        total = col_buf[it, 0]
        for q in range(1, n_z):
            total = total + col_buf[it, q]
        crow_ref[...] = 1.0 / total

        @pl.loop(0, tokens // 64, unroll=2)
        def _(i):
            rows = pl.ds(pl.multiple_of(i * 64, 64), 64)
            running = e_ref[rows, 0:LANES] * crow_ref[:, 0:LANES]
            for t in range(1, protos // LANES):
                cols = slice(t * LANES, (t + 1) * LANES)
                running = running + e_ref[rows, cols] * crow_ref[:, cols]
            acc_ref[rows, :] = running

        row_buf[it, me_p, 0:1, :] = lane_sums(acc_ref)
        row_buf[it, me_p, 1:2, :] = student_row
        copies = row_copies(it)
        start(copies)
        if it == ITERS - 1:
            cb_ref[...] = as_columns(crow_ref[...])
        wait(copies)
        if it == 1:
            wait(t2[0])
            start(t3[0])
        if it < 2:
            wait(t1[it])
            start(t2[it])
        total = row_buf[it, 0]
        for q in range(1, n_p):
            total = total + row_buf[it, q]
        row_scale = row_scale / (row_scale * total[0:1, :])
        if it == 0:
            student_total = total[1:2, :]
        if it < ITERS - 1:
            rb_ref[...] = as_columns(row_scale)

    gain = weight[...].reshape(1, tokens) / TEMP_STUDENT
    student_gain = gain / student_total
    teacher_gain = gain * row_scale
    fac_buf[me_z, 0:1, :] = student_gain
    fac_buf[me_z, 1:2, :] = teacher_gain
    mine = fac_buf.at[me_z]
    fac = [
        remote(mine, mine, fac_send.at[j - 1], fac_recv.at[j - 1], me_p, (me_z + j) % n_z)
        for j in range(1, n_z)
    ]
    start(fac)
    wait(t2[1])
    start(t3[1])

    rb_ref[...] = as_columns(teacher_gain)
    ab_ref[...] = as_columns(student_gain)

    def feature_rows(first, count):
        rows = pl.ds(pl.multiple_of(first, 16), count)
        a = ab_ref[rows, :]
        b = rb_ref[rows, :]
        parts = []
        for t in range(protos // LANES):
            cols = slice(t * LANES, (t + 1) * LANES)
            parts.append(
                (s_ref[rows, cols] * a - e_ref[rows, cols] * b * crow_ref[:, cols]).astype(BF16)
            )
        feat[rows, :] = dot_nn(jnp.concatenate(parts, axis=1), ph[...])
        return rows

    quarter = tokens // 4
    theirs = ((g + 1) % 2) * (tokens // 2)
    ours = (g % 2) * (tokens // 2)
    pair = []
    for i in range(2):
        rows = feature_rows(theirs + i * quarter, quarter)
        pair.append(remote(
            feat.at[rows, :], pair_buf.at[i], pair_send.at[i], pair_recv.at[i], other, me_z,
        ))
        start(pair[i:])
    for i in range(2):
        feature_rows(ours + i * quarter, quarter)


    def proto_tile(i):
        rows = pl.ds(pl.multiple_of(i * WIDE, WIDE), WIDE)
        p_half = ph[rows, :]
        q_half = qh[rows, :]
        c = jnp.concatenate([cb_ref[rows, :]] * (CHUNK // LANES), axis=1)

        def block(k, running):
            part = pl.ds(pl.multiple_of(k * CHUNK, CHUNK), CHUNK)
            student = tok_s[part, :]
            prob = jnp.exp2(dot_nt(p_half, student) * STUDENT_RATE)
            target = jnp.exp2(dot_nt(q_half, tok_t[part, :]) * TEACHER_RATE)
            coefficient = prob * fac_flat[0:1, part] - target * fac_flat[1:2, part] * c
            return running + dot_nn(coefficient.astype(BF16), student)

        total = jnp.zeros((WIDE, dim), F32)
        chunks = n_z * tokens // CHUNK
        if chunks <= 5:
            for k in range(chunks):
                total = block(k, total)
        else:
            total = lax.fori_loop(0, chunks, block, total)
        values = pp[rows, :].astype(F32)
        norm = row_norm(values)
        unit = values / norm
        inner = jnp.sum(total * unit, axis=1, keepdims=True)
        proto_out[rows, :] = ((total - inner * unit) / norm).astype(BF16)

    tiles = protos // WIDE
    wait(pair)
    for i in range(2):
        rows = pl.ds(pl.multiple_of(ours + i * quarter, 16), quarter)
        feat[rows, :] += pair_buf[i]
    rs = []
    for j in range(1, GROUP // 2):
        to = (g + 2 * j) % GROUP
        rs.append(remote(
            feat.at[pl.ds(rows_of(to), share), :], rs_buf.at[j - 1],
            rs_send.at[j - 1], rs_recv.at[j - 1], octet * GROUP + to, me_z,
        ))
    start(rs)
    wait(fac)
    wait(t3[0])
    wait(t3[1])
    for z in range(n_z):
        fac_flat[:, z * tokens:(z + 1) * tokens] = fac_buf[z]
    early = tiles // 2
    pl.loop(0, early)(proto_tile)

    wait(rs)
    own = pl.ds(rows_of(g), share)
    total = feat[own, :]
    for j in range(1, GROUP // 2):
        total = total + rs_buf[j - 1]
    if octets > 1:
        rs2_buf[octet] = total
        mine2 = rs2_buf.at[octet]
        rs2 = [
            remote(mine2, mine2, rs2_send.at[j - 1], rs2_recv.at[j - 1],
                   ((octet + j) % octets) * GROUP + g, me_z)
            for j in range(1, octets)
        ]
        start(rs2)
        wait(rs2)
        total = rs2_buf[0]
        for q in range(1, octets):
            total = total + rs2_buf[q]
    unit = s_unit[own, :]
    inner = jnp.sum(total * unit, axis=1, keepdims=True)
    norm = jnp.concatenate([s_norm[own, :]] * (dim // LANES), axis=1)
    fgrad[own, :] = ((total - inner * unit) / norm).astype(BF16)
    piece = fgrad.at[own, :]
    ag = [
        remote(piece, piece, ag_send.at[j - 1], ag_recv.at[j - 1],
               octet * GROUP + (g + j) % GROUP, me_z)
        for j in range(1, GROUP)
    ]
    start(ag)

    pl.loop(early, tiles)(proto_tile)

    wait(ag)
    for copy in pending:
        copy.wait_send()

    @pl.loop(0, patches // TILE, unroll=True)
    def _(i):
        rows = pl.ds(pl.multiple_of(i * TILE, TILE), TILE)
        patch_out[rows, :] = dot_nn(hot_t[rows, :], fgrad[...]).astype(BF16)


def body(n_p, n_z, sp, tp, positions, weight, pp, qp):
    patches, dim = sp.shape
    tokens = positions.shape[0]
    protos = pp.shape[0]
    share = tokens // GROUP
    octets = n_p // GROUP
    vmem = pltpu.VMEM
    dma = pltpu.SemaphoreType.DMA
    one = max(octets - 1, 1)
    scratch = [
        vmem((protos, dim), BF16),
        vmem((protos, dim), BF16),
        dma((2,)),
        vmem((tokens, patches), BF16),
        vmem((patches, tokens), BF16),
        vmem((n_z * tokens, dim), BF16),
        vmem((n_z * tokens, dim), BF16),
        vmem((2, n_z * tokens), F32),
        vmem((tokens, dim), F32),
        vmem((tokens, LANES), F32),
        vmem((protos, dim), BF16),
        vmem((protos, dim), BF16),
        vmem((tokens, protos), F32),
        vmem((tokens, protos), F32),
        vmem((tokens, LANES), F32),
        vmem((tokens, LANES), F32),
        vmem((tokens, LANES), F32),
        vmem((tokens, LANES), F32),
        vmem((protos, LANES), F32),
        vmem((1, protos), F32),
        vmem((ITERS, n_p, 2, tokens), F32),
        vmem((ITERS, n_z, 1, protos), F32),
        vmem((n_z, 2, tokens), F32),
        vmem((tokens, dim), F32),
        vmem((2, tokens // 4, dim), F32),
        vmem((GROUP // 2 - 1, share, dim), F32),
        vmem((octets, share, dim), F32),
        vmem((tokens, dim), BF16),
        dma((ITERS, n_p - 1)), dma((ITERS, n_p - 1)),
        dma((ITERS, n_z - 1)), dma((ITERS, n_z - 1)),
        dma((n_z - 1,)), dma((n_z - 1,)),
        dma((2, n_z - 1)), dma((2, n_z - 1)),
        dma((2, n_z - 1, GROUP // 2 - 1)), dma((2, n_z - 1, GROUP // 2 - 1)),
        dma((2, n_z - 1)), dma((2, n_z - 1)),
        dma((2,)), dma((2,)),
        dma((GROUP // 2 - 1,)), dma((GROUP // 2 - 1,)),
        dma((one,)), dma((one,)),
        dma((GROUP - 1,)), dma((GROUP - 1,)),
    ]
    spec = pl.BlockSpec(memory_space=pltpu.VMEM)
    return pl.pallas_call(
        functools.partial(kernel, n_p, n_z),
        out_shape=(
            jax.ShapeDtypeStruct((patches, dim), BF16),
            jax.ShapeDtypeStruct((protos, dim), BF16),
        ),
        in_specs=[spec] * 4 + [pl.BlockSpec(memory_space=pl.ANY)] * 2,
        out_specs=(spec, spec),
        scratch_shapes=scratch,
        compiler_params=pltpu.CompilerParams(
            collective_id=0, has_side_effects=True, vmem_limit_bytes=58 * 1024 * 1024
        ),
    )(sp, tp, positions, weight, pp, qp)


def solution(mesh):
    return jax.shard_map(
        functools.partial(body, mesh.shape["proto"], mesh.shape["batch"]),
        mesh=mesh,
        in_specs=(
            P("batch", None),
            P("batch", None),
            P("batch"),
            P("batch"),
            P("proto", None),
            P("proto", None),
        ),
        out_specs=(P("batch", None), P("proto", None)),
        check_vma=False,
    )
```
